32 devices in a mesh: grp: 2 (over core), req: 16 (over z, y, x).
Axes of the slice: x: 2, y: 2, z: 4, core: 2. Of those that a mesh axis runs over, the one named last changes fastest.
Arguments:
- new_qkv: bfloat16 [128, 32, 3840], P(('grp', 'req')), parts along dimension 0, may hold values from -5 to 5
- cache_kv: bfloat16 [128, 32, 2560], P(('grp', 'req')), parts along dimension 0, may hold values from -5 to 5
- resid: bfloat16 [128, 32, 1280], P(('grp', 'req')), parts along dimension 0, may hold values from -6 to 6
- span_len: int32 [128], P(('grp', 'req')), parts along dimension 0, may hold values from 1 to 32
- cache_len: int32 [128], P(('grp', 'req')), parts along dimension 0, may hold values from 0 to 32
- series_perm: int32 [128], P(('grp', 'req')), parts along dimension 0, may hold values from 0 to 63, each once
- ff_gain: float32 [1280], replicated, may hold values from 0.5 to 1.5
- w_up: bfloat16 [1280, 1280], replicated, may hold values from -0.15625 to 0.15625
- w_down: bfloat16 [1280, 1280], replicated, may hold values from -0.15625 to 0.15625
Outputs:
- packed_out: bfloat16 [4096, 1280], P(('grp', 'req')), parts along dimension 0
The draws below stay inside these ranges and needn't reach their ends.
There are 2 independent parts, one for each index of `grp`. The reference program is written for one: setup_inputs(seed, part) draws one part's arguments, and reference() takes and returns one part's arrays. A program takes and returns all parts, laid end to end along the dimension named above; an argument that names none is the same for every part. Nothing has to cross between parts.
Inputs may be any that keep to these rules, and one draw needn't show every extreme that they name: `series_perm`: each series id appears once.
All inputs are finite; a program needn't handle non-finite values.
Results may differ from the reference program's by a relative error of at most 0.0055.
Values may be sent and summed in bfloat16 or wider, within the bound.
A program may use at most 64 MiB of HBM per device.

```python
import jax
import jax.numpy as jnp
from jax import lax

D = 1280
H = 16
HD = 80
FF = 1280
S_DEV = 4
SPAN = 32
CACHE = 32
SERIES = 64
TOKCAP = 2048
N_REQ = 16


def draw_new_qkv(key, part):
    base_key = jax.random.fold_in(key, 1)
    base = jnp.clip(jax.random.normal(base_key, (SERIES, SPAN, 3 * D), jnp.float32), -4.5, 4.5)
    return base.astype(jnp.bfloat16)


def draw_cache_kv(key, part):
    base_key = jax.random.fold_in(key, 2)
    base = jnp.clip(jax.random.normal(base_key, (SERIES, CACHE, 2 * D), jnp.float32), -4.5, 4.5)
    return base.astype(jnp.bfloat16)


def draw_span_len(key, part):
    key_len, key_pick = jax.random.split(jax.random.fold_in(key, 3))
    lengths = jax.random.randint(key_len, (SERIES,), 1, SPAN + 1)
    picked = jax.random.randint(key_pick, (), 0, SERIES)
    lengths = lengths.at[picked].set(SPAN)
    lengths = lengths.at[(picked + 1) % SERIES].set(1)
    return lengths.astype(jnp.int32)


def draw_cache_len(key, part):
    key_len, key_pick = jax.random.split(jax.random.fold_in(key, 4))
    lengths = jax.random.randint(key_len, (SERIES,), 0, CACHE + 1)
    picked = jax.random.randint(key_pick, (), 0, SERIES)
    lengths = lengths.at[picked].set(CACHE)
    lengths = lengths.at[(picked + 1) % SERIES].set(0)
    return lengths.astype(jnp.int32)


def block_scale(key, dims, cuts, smallest, high):
    loudness = 1.0
    for axis_at, shards_of in cuts:
        steps = jax.random.uniform(jax.random.fold_in(jax.random.fold_in(key, 6), axis_at), (shards_of,), jnp.float32, smallest / len(cuts), high / len(cuts))
        loudness = loudness * jnp.repeat(jnp.exp(steps), dims[axis_at] // shards_of).reshape((-1,) + (1,) * (len(dims) - 1 - axis_at))
    return loudness


def normal_values(stream_key, extent, spread, limit, cuts=(), kind=jnp.bfloat16):
    entries = spread * jax.random.normal(stream_key, extent, jnp.float32)
    if cuts:
        entries = entries * block_scale(stream_key, extent, cuts, -0.22, 0.18)
    return jnp.clip(entries, -limit, limit).astype(kind)


def setup_inputs(seed: int = 0, part: int = 0) -> dict:
    splits = jax.random.split(jax.random.key(seed), 10)
    part_keys = jax.random.split(jax.random.fold_in(splits[9], part), 10)
    return {
        "new_qkv": draw_new_qkv(jax.random.fold_in(jax.random.fold_in(splits[9], part), 71), part),
        "cache_kv": draw_cache_kv(jax.random.fold_in(jax.random.fold_in(splits[9], part), 71), part),
        "resid": normal_values(part_keys[2], (SERIES, SPAN, D), 1.0, 6.0, ((0, 16),)),
        "span_len": draw_span_len(jax.random.fold_in(jax.random.fold_in(splits[9], part), 71), part),
        "cache_len": draw_cache_len(jax.random.fold_in(jax.random.fold_in(splits[9], part), 71), part),
        "series_perm": jax.random.permutation(part_keys[5], SERIES).astype(jnp.int32),
        "ff_gain": jnp.clip(jax.random.uniform(splits[6], (D,), jnp.float32, 0.5, 1.5), 0.5, 1.5),
        "w_up": normal_values(splits[7], (D, FF), D ** -0.5, 0.15625),
        "w_down": normal_values(splits[8], (FF, D), FF ** -0.5, 0.15625),
    }


def attend_series(series_args):
    new_rows, cached, new_count, cached_count = series_args
    queries = new_rows[:, :D].astype(jnp.float32).reshape(SPAN, H, HD)
    key_rows = jnp.concatenate([cached[:, :D], new_rows[:, D:2 * D]], axis=0).astype(jnp.float32).reshape(CACHE + SPAN, H, HD)
    value_rows = jnp.concatenate([cached[:, D:], new_rows[:, 2 * D:]], axis=0).astype(jnp.float32).reshape(CACHE + SPAN, H, HD)
    scores = jnp.einsum('thd,khd->htk', queries, key_rows) * HD ** (-0.5)
    key_pos = jnp.arange(CACHE + SPAN, dtype=jnp.int32)[None, :]
    row_pos = jnp.arange(SPAN, dtype=jnp.int32)[:, None]
    visible = jnp.where(key_pos < CACHE, key_pos < cached_count, key_pos - CACHE <= row_pos)
    scores = jnp.where(visible[None], scores, -1e+30)
    row_top = lax.optimization_barrier(jnp.max(scores, axis=-1, keepdims=True))
    expo_terms = jnp.exp(scores - row_top)
    weights = expo_terms / lax.optimization_barrier(jnp.sum(expo_terms, axis=-1, keepdims=True))
    weights = lax.optimization_barrier(weights.astype(jnp.bfloat16)).astype(jnp.float32)
    attended = jnp.einsum('htk,khd->thd', weights, value_rows)
    return attended.reshape(SPAN, D)

def feed_forward(hidden, ff_gain, w_up, w_down):
    wide_rows = hidden.astype(jnp.float32)
    normed = (wide_rows * lax.rsqrt(lax.optimization_barrier(jnp.mean(wide_rows * wide_rows, axis=-1, keepdims=True)) + 1e-06) * ff_gain).astype(jnp.bfloat16)
    activated = jax.nn.silu(jnp.dot(normed, w_up, preferred_element_type=jnp.float32)).astype(jnp.bfloat16)
    return (wide_rows + jnp.dot(activated, w_down, preferred_element_type=jnp.float32)).astype(jnp.bfloat16)

def reference(new_qkv, cache_kv, resid, span_len, cache_len, series_perm, ff_gain, w_up, w_down):
    attended = lax.map(attend_series, (new_qkv, cache_kv, span_len, cache_len))
    hidden = (resid.astype(jnp.float32) + attended).astype(jnp.bfloat16)
    count_by_id = jnp.zeros((SERIES,), jnp.int32).at[series_perm].set(span_len)
    start_by_id = (jnp.cumsum(count_by_id) - count_by_id).astype(jnp.int32)
    slot_index = jnp.arange(SPAN, dtype=jnp.int32)
    packed_index = (start_by_id[series_perm][:, None] + slot_index[None, :]).astype(jnp.int32)
    live_slot = slot_index[None, :] < span_len[:, None]
    out_row = packed_index % N_REQ * (S_DEV * SPAN) + packed_index // N_REQ
    out_row = jnp.where(live_slot, out_row, TOKCAP).astype(jnp.int32).reshape(-1)
    layer_out = feed_forward(hidden.reshape(SERIES * SPAN, D), ff_gain, w_up, w_down)
    packed_out = jnp.zeros((TOKCAP, D), jnp.bfloat16).at[out_row].set(layer_out, mode='drop')
    return packed_out
```

```python
import functools

import jax
import jax.numpy as jnp
from jax import lax
from jax.experimental import pallas as pl
from jax.experimental.pallas import tpu as pltpu
from jax.sharding import PartitionSpec as P

H = 16
LANES = 128
ROWS = 8
CUTS = (512, 1280)
HEAD_CUTS = (8, 16)


def div(x, k):
    return lax.shift_right_arithmetic(x, jnp.int32(k.bit_length() - 1)) if k & (k - 1) == 0 else x // k


def mod(x, k):
    return x & (k - 1) if k & (k - 1) == 0 else x % k


def windows(heads, head_size):
    found = []
    for h in heads:
        if found and (h + 1) * head_size <= found[-1][0] + 2 * LANES:
            found[-1][1].append(h)
        else:
            found.append((h * head_size // LANES * LANES, [h]))
    return found


def kernel(
    n, series, span, cache, width,
    qkv_hbm, cache_hbm, resid_hbm, len_ref, clen_ref, perm_ref, gain_ref, up_hbm, down_hbm,
    out_ref,
    qkv, ckv, resid, w_up, w_down, hid, act, meta_send, meta, sends, recvs,
    load_sem, meta_ssem, meta_rsem, ssems, rsems,
):
    me = lax.axis_index("req")
    head_size = width // H
    per = (span + n - 1) // n
    rows_here = series * span
    tiles = n * ROWS // LANES
    group = LANES // ROWS

    loads = [
        pltpu.make_async_copy(src, dst, load_sem.at[k])
        for k, (src, dst) in enumerate(
            ((qkv_hbm, qkv), (cache_hbm, ckv), (resid_hbm, resid), (up_hbm, w_up), (down_hbm, w_down))
        )
    ]
    for load in loads:
        load.start()

    barrier = pltpu.get_barrier_semaphore()

    @pl.loop(1, n)
    def _(k):
        pl.semaphore_signal(
            barrier, inc=1, device_id={"req": lax.rem(me + k, n)}, device_id_type=pl.DeviceIdType.MESH
        )

    sub = lax.broadcasted_iota(jnp.int32, (ROWS, LANES), 0)
    lens = jnp.zeros((ROWS, LANES), jnp.int32)
    ids = jnp.zeros((ROWS, LANES), jnp.int32)
    for i in range(series):
        lens = jnp.where(sub == i, len_ref[i], lens)
        ids = jnp.where(sub == i, perm_ref[i], ids)
    meta_send[0:ROWS] = lens
    meta_send[ROWS:] = ids
    meta[me] = meta_send[...]
    pl.semaphore_wait(barrier, n - 1)

    def meta_copy(peer, slot):
        return pltpu.make_async_remote_copy(
            src_ref=meta_send, dst_ref=meta.at[slot], send_sem=meta_ssem.at[peer], recv_sem=meta_rsem.at[slot],
            device_id={"req": peer}, device_id_type=pl.DeviceIdType.MESH,
        )

    @pl.loop(1, n)
    def _(k):
        meta_copy(lax.rem(me + k, n), me).start()

    for load in loads[:3]:
        load.wait()

    lane = lax.broadcasted_iota(jnp.int32, (1, 2 * LANES), 1)
    key_pos = lax.broadcasted_iota(jnp.int32, (span, cache + span), 1)
    row_pos = lax.broadcasted_iota(jnp.int32, (span, cache + span), 0)

    def attend(heads):
        wins = windows(heads, head_size)
        first, last = heads[0] * head_size, (heads[-1] + 1) * head_size

        @pl.loop(0, series)
        def _(i):
            limit = clen_ref[i]
            visible = (key_pos < limit) | ((key_pos >= cache) & (key_pos - cache <= row_pos))
            parts = {}
            for base, group_heads in wins:
                wide = min(2 * LANES, width - base)
                masks = [
                    jnp.where(
                        (lane[:, :wide] >= h * head_size - base) & (lane[:, :wide] < (h + 1) * head_size - base),
                        1.0, 0.0,
                    )
                    for h in group_heads
                ]
                q = qkv[i, :, base : base + wide]
                qs = jnp.concatenate([q * m.astype(jnp.bfloat16) for m in masks], axis=0)
                keys = jnp.concatenate(
                    [ckv[i, :, base : base + wide], qkv[i, :, width + base : width + base + wide]], axis=0
                )
                values = jnp.concatenate(
                    [ckv[i, :, width + base : width + base + wide],
                     qkv[i, :, 2 * width + base : 2 * width + base + wide]], axis=0
                )
                s = lax.dot_general(qs, keys, (((1,), (1,)), ((), ())), preferred_element_type=jnp.float32)
                s = s.reshape(len(masks), span, cache + span) * head_size ** (-0.5)
                s = jnp.where(visible[None], s, -1e30)
                e = jnp.exp(s - jnp.max(s, axis=-1, keepdims=True))
                w = (e * (1.0 / jnp.sum(e, axis=-1, keepdims=True))).astype(jnp.bfloat16)
                o = jnp.dot(
                    w.reshape(len(masks) * span, cache + span), values, preferred_element_type=jnp.float32
                )
                total = sum(o[k * span : (k + 1) * span] * m for k, m in enumerate(masks))
                for at in range(0, wide, LANES):
                    piece = total[:, at : at + LANES]
                    parts[base + at] = parts[base + at] + piece if base + at in parts else piece
            for at, piece in parts.items():
                if first <= at and at + LANES <= last:
                    hid[pl.ds(pl.multiple_of(i * span, span), span), at : at + LANES] = (
                        resid[i, :, at : at + LANES].astype(jnp.float32) + piece
                    ).astype(jnp.bfloat16)

    lane1 = lax.broadcasted_iota(jnp.int32, (1, LANES), 1)

    def starts_of(ids_of_lanes):
        earlier = jnp.where(meta[:, ROWS:, :] < ids_of_lanes[None], meta[:, :ROWS, :], 0)
        return jnp.sum(jnp.sum(earlier, axis=0), axis=0, keepdims=True)

    def block_copy(c, peer, slot):
        return pltpu.make_async_remote_copy(
            src_ref=sends[c].at[peer], dst_ref=recvs[c].at[slot], send_sem=ssems.at[c, peer],
            recv_sem=rsems.at[c, slot], device_id={"req": peer}, device_id_type=pl.DeviceIdType.MESH,
        )

    place = None
    done = 0
    for c, (head_end, cut) in enumerate(zip(HEAD_CUTS, CUTS)):
        attend(list(range(HEAD_CUTS[c - 1] if c else 0, head_end)))
        if c == 0:
            @pl.loop(1, n)
            def _(k):
                src = lax.rem(me + n - k, n)
                meta_copy(src, src).wait_recv()

            own_ids = jnp.zeros((1, rows_here), jnp.int32)
            own_len = jnp.zeros((1, rows_here), jnp.int32)
            token = lax.broadcasted_iota(jnp.int32, (1, rows_here), 1)
            own = div(token, span)
            slot = mod(token, span)
            for i in range(series):
                own_ids = jnp.where(own == i, perm_ref[i], own_ids)
                own_len = jnp.where(own == i, len_ref[i], own_len)
            at = mod(starts_of(own_ids) + slot, n) * ROWS + own * per + div(slot, n)
            place = jnp.where(slot < own_len, at, -1)
        half = (cut - done) // 2
        rows = lax.broadcasted_iota(jnp.int32, (LANES, rows_here), 0)
        for k in range(tiles):
            pick = jnp.where(rows + k * LANES == place, 1.0, 0.0).astype(jnp.bfloat16)
            moved = jnp.dot(pick, hid[:, done:cut], preferred_element_type=jnp.float32)
            moved = jnp.concatenate(
                [moved[:, :half].reshape(group, ROWS, half), moved[:, half:].reshape(group, ROWS, half)], axis=1
            )
            sends[c][k * group : (k + 1) * group] = moved.astype(jnp.bfloat16)

        @pl.loop(1, n)
        def _(k, c=c):
            block_copy(c, lax.rem(me + k, n), me).start()

        recvs[c][me] = sends[c][me]
        done = cut

    sub = lax.broadcasted_iota(jnp.int32, (ROWS, LANES), 0)
    lane8 = lax.broadcasted_iota(jnp.int32, (ROWS, LANES), 1)
    local = []
    for k in range(tiles):
        a_ids = jnp.zeros((ROWS, LANES), jnp.int32)
        a_len = jnp.zeros((ROWS, LANES), jnp.int32)
        for s in range(group):
            mine = (div(lane8, ROWS) == s) & (div(mod(lane8, ROWS), per) == sub)
            a_ids = jnp.where(mine, meta[k * group + s, ROWS:, :], a_ids)
            a_len = jnp.where(mine, meta[k * group + s, :ROWS, :], a_len)
        a_ids = jnp.sum(a_ids, axis=0, keepdims=True)
        a_len = jnp.sum(a_len, axis=0, keepdims=True)
        begin = starts_of(a_ids)
        t = mod(me - begin, n) + n * mod(lane1, per)
        local.append(jnp.where(t < a_len, div(begin + t, n), -1))

    out_rows = lax.broadcasted_iota(jnp.int32, (rows_here, LANES), 0)
    picks = [jnp.where(out_rows == spot, 1.0, 0.0).astype(jnp.bfloat16) for spot in local]
    wide = []
    for c in range(len(CUTS)):
        @pl.loop(1, n)
        def _(k, c=c):
            src = lax.rem(me + n - k, n)
            block_copy(c, src, src).wait_recv()

        total = None
        for k in range(tiles):
            got = recvs[c][k * group : (k + 1) * group].astype(jnp.float32)
            half = got.shape[2]
            got = jnp.concatenate(
                [got[:, :ROWS].reshape(LANES, half), got[:, ROWS:].reshape(LANES, half)], axis=1
            ).astype(jnp.bfloat16)
            more = jnp.dot(picks[k], got, preferred_element_type=jnp.float32)
            total = more if total is None else total + more
        wide.append(total)
    hidden = jnp.concatenate(wide, axis=1)
    normed = (
        hidden * lax.rsqrt(jnp.mean(hidden * hidden, axis=-1, keepdims=True) + 1e-06) * gain_ref[...]
    ).astype(jnp.bfloat16)
    loads[3].wait()
    step = 256
    for at in range(0, w_up.shape[1], step):
        v = jnp.dot(normed, w_up[:, at : at + step], preferred_element_type=jnp.float32)
        act[:, at : at + step] = (v * (1.0 / (1.0 + jnp.exp(-v)))).astype(jnp.bfloat16)
    loads[4].wait()
    for at in range(0, width, step):
        v = jnp.dot(act[...], w_down[:, at : at + step], preferred_element_type=jnp.float32)
        out_ref[:, at : at + step] = (hidden[:, at : at + step] + v).astype(jnp.bfloat16)

    @pl.loop(1, n)
    def _(k):
        peer = lax.rem(me + k, n)
        meta_copy(peer, me).wait_send()
        for c in range(len(CUTS)):
            block_copy(c, peer, me).wait_send()


def local(new_qkv, cache_kv, resid, span_len, cache_len, series_perm, ff_gain, w_up, w_down):
    n = lax.axis_size("req")
    series, span, _ = new_qkv.shape
    cache, width, hidden = cache_kv.shape[1], resid.shape[2], w_up.shape[1]
    rows_here = series * span
    halves = [(b - a) // 2 for a, b in zip((0,) + CUTS, CUTS)]
    hbm, smem, vmem = (pl.BlockSpec(memory_space=m) for m in (pl.ANY, pltpu.SMEM, pltpu.VMEM))
    return pl.pallas_call(
        functools.partial(kernel, n, series, span, cache, width),
        out_shape=jax.ShapeDtypeStruct((rows_here, width), jnp.bfloat16),
        in_specs=[hbm, hbm, hbm, smem, smem, smem, vmem, hbm, hbm],
        out_specs=vmem,
        scratch_shapes=[
            pltpu.VMEM(new_qkv.shape, jnp.bfloat16),
            pltpu.VMEM(cache_kv.shape, jnp.bfloat16),
            pltpu.VMEM(resid.shape, jnp.bfloat16),
            pltpu.VMEM(w_up.shape, jnp.bfloat16),
            pltpu.VMEM(w_down.shape, jnp.bfloat16),
            pltpu.VMEM((rows_here, width), jnp.bfloat16),
            pltpu.VMEM((rows_here, hidden), jnp.bfloat16),
            pltpu.VMEM((2 * ROWS, LANES), jnp.int32),
            pltpu.VMEM((n, 2 * ROWS, LANES), jnp.int32),
            [pltpu.VMEM((n, 2 * ROWS, h), jnp.bfloat16) for h in halves],
            [pltpu.VMEM((n, 2 * ROWS, h), jnp.bfloat16) for h in halves],
            pltpu.SemaphoreType.DMA((5,)),
            pltpu.SemaphoreType.DMA((n,)),
            pltpu.SemaphoreType.DMA((n,)),
            pltpu.SemaphoreType.DMA((len(CUTS), n)),
            pltpu.SemaphoreType.DMA((len(CUTS), n)),
        ],
        compiler_params=pltpu.CompilerParams(
            collective_id=0, has_side_effects=True, vmem_limit_bytes=40 * 2**20
        ),
    )(new_qkv, cache_kv, resid, span_len, cache_len, series_perm, ff_gain.reshape(1, -1), w_up, w_down)


def solution(mesh):
    rows3, rows1 = P(("grp", "req"), None, None), P(("grp", "req"))
    in_specs = (rows3, rows3, rows3, rows1, rows1, rows1, P(), P(), P())
    out_specs = P(("grp", "req"), None)
    return jax.shard_map(local, mesh=mesh, in_specs=in_specs, out_specs=out_specs, check_vma=False)
```

```python
import functools

import jax
import jax.numpy as jnp
from jax import lax
from jax.experimental import pallas as pl
from jax.experimental.pallas import tpu as pltpu
from jax.sharding import PartitionSpec as P

H = 16
LANES = 128
ROWS = 8
CUTS = (512, 1280)
HEAD_CUTS = (8, 16)


def div(x, k):
    return lax.shift_right_arithmetic(x, jnp.int32(k.bit_length() - 1)) if k & (k - 1) == 0 else x // k


def mod(x, k):
    return x & (k - 1) if k & (k - 1) == 0 else x % k


def windows(heads, head_size):
    found = []
    for h in heads:
        if found and (h + 1) * head_size <= found[-1][0] + 2 * LANES:
            found[-1][1].append(h)
        else:
            found.append((h * head_size // LANES * LANES, [h]))
    return found


def kernel(
    n, series, span, cache, width,
    qkv_hbm, cache_hbm, resid_hbm, len_hbm, clen_hbm, perm_hbm, gain_hbm, up_hbm, down_hbm,
    out_ref,
    qkv, ckv, resid, len_ref, clen_ref, perm_ref, gain, w_up, w_down, hid, act, meta_send, meta, sends, recvs,
    load_sem, meta_ssem, meta_rsem, ssems, rsems,
):
    me = lax.axis_index("req")
    head_size = width // H
    per = (span + n - 1) // n
    rows_here = series * span
    tiles = n * ROWS // LANES
    group = LANES // ROWS

    loads = [
        pltpu.make_async_copy(src, dst, load_sem.at[k])
        for k, (src, dst) in enumerate(
            (
                (len_hbm, len_ref), (perm_hbm, perm_ref), (clen_hbm, clen_ref), (qkv_hbm, qkv), (cache_hbm, ckv),
                (resid_hbm, resid), (gain_hbm, gain), (up_hbm, w_up), (down_hbm, w_down),
            )
        )
    ]
    barrier = pltpu.get_barrier_semaphore()

    @pl.loop(1, n)
    def _(k):
        pl.semaphore_signal(
            barrier, inc=1, device_id={"req": lax.rem(me + k, n)}, device_id_type=pl.DeviceIdType.MESH
        )

    for load in loads:
        load.start()
    for load in loads[:2]:
        load.wait()

    sub = lax.broadcasted_iota(jnp.int32, (ROWS, LANES), 0)
    lens = jnp.zeros((ROWS, LANES), jnp.int32)
    ids = jnp.zeros((ROWS, LANES), jnp.int32)
    for i in range(series):
        lens = jnp.where(sub == i, len_ref[i], lens)
        ids = jnp.where(sub == i, perm_ref[i], ids)
    meta_send[0:ROWS] = lens
    meta_send[ROWS:] = ids
    meta[me] = meta_send[...]
    pl.semaphore_wait(barrier, n - 1)

    def meta_copy(peer, slot):
        return pltpu.make_async_remote_copy(
            src_ref=meta_send, dst_ref=meta.at[slot], send_sem=meta_ssem.at[peer], recv_sem=meta_rsem.at[slot],
            device_id={"req": peer}, device_id_type=pl.DeviceIdType.MESH,
        )

    @pl.loop(1, n)
    def _(k):
        meta_copy(lax.rem(me + k, n), me).start()

    for load in loads[2:6]:
        load.wait()

    lane = lax.broadcasted_iota(jnp.int32, (1, 2 * LANES), 1)
    key_pos = lax.broadcasted_iota(jnp.int32, (span, cache + span), 1)
    row_pos = lax.broadcasted_iota(jnp.int32, (span, cache + span), 0)

    def attend(heads):
        wins = windows(heads, head_size)
        first, last = heads[0] * head_size, (heads[-1] + 1) * head_size

        @pl.loop(0, series)
        def _(i):
            limit = clen_ref[i]
            visible = (key_pos < limit) | ((key_pos >= cache) & (key_pos - cache <= row_pos))
            parts = {}
            for base, group_heads in wins:
                wide = min(2 * LANES, width - base)
                masks = [
                    jnp.where(
                        (lane[:, :wide] >= h * head_size - base) & (lane[:, :wide] < (h + 1) * head_size - base),
                        1.0, 0.0,
                    )
                    for h in group_heads
                ]
                q = qkv[i, :, base : base + wide]
                qs = jnp.concatenate([q * m.astype(jnp.bfloat16) for m in masks], axis=0)
                keys = jnp.concatenate(
                    [ckv[i, :, base : base + wide], qkv[i, :, width + base : width + base + wide]], axis=0
                )
                values = jnp.concatenate(
                    [ckv[i, :, width + base : width + base + wide],
                     qkv[i, :, 2 * width + base : 2 * width + base + wide]], axis=0
                )
                s = lax.dot_general(qs, keys, (((1,), (1,)), ((), ())), preferred_element_type=jnp.float32)
                s = s.reshape(len(masks), span, cache + span) * head_size ** (-0.5)
                s = jnp.where(visible[None], s, -1e30)
                e = jnp.exp(s - jnp.max(s, axis=-1, keepdims=True))
                w = (e * (1.0 / jnp.sum(e, axis=-1, keepdims=True))).astype(jnp.bfloat16)
                o = jnp.dot(
                    w.reshape(len(masks) * span, cache + span), values, preferred_element_type=jnp.float32
                )
                total = sum(o[k * span : (k + 1) * span] * m for k, m in enumerate(masks))
                for at in range(0, wide, LANES):
                    piece = total[:, at : at + LANES]
                    parts[base + at] = parts[base + at] + piece if base + at in parts else piece
            for at, piece in parts.items():
                if first <= at and at + LANES <= last:
                    hid[pl.ds(pl.multiple_of(i * span, span), span), at : at + LANES] = (
                        resid[i, :, at : at + LANES].astype(jnp.float32) + piece
                    ).astype(jnp.bfloat16)

    lane1 = lax.broadcasted_iota(jnp.int32, (1, LANES), 1)

    def starts_of(ids_of_lanes):
        earlier = jnp.where(meta[:, ROWS:, :] < ids_of_lanes[None], meta[:, :ROWS, :], 0)
        return jnp.sum(jnp.sum(earlier, axis=0), axis=0, keepdims=True)

    def block_copy(c, peer, slot):
        return pltpu.make_async_remote_copy(
            src_ref=sends[c].at[peer], dst_ref=recvs[c].at[slot], send_sem=ssems.at[c, peer],
            recv_sem=rsems.at[c, slot], device_id={"req": peer}, device_id_type=pl.DeviceIdType.MESH,
        )

    place = None
    done = 0
    for c, (head_end, cut) in enumerate(zip(HEAD_CUTS, CUTS)):
        attend(list(range(HEAD_CUTS[c - 1] if c else 0, head_end)))
        if c == 0:
            @pl.loop(1, n)
            def _(k):
                src = lax.rem(me + n - k, n)
                meta_copy(src, src).wait_recv()

            own_ids = jnp.zeros((1, rows_here), jnp.int32)
            own_len = jnp.zeros((1, rows_here), jnp.int32)
            token = lax.broadcasted_iota(jnp.int32, (1, rows_here), 1)
            own = div(token, span)
            slot = mod(token, span)
            for i in range(series):
                own_ids = jnp.where(own == i, perm_ref[i], own_ids)
                own_len = jnp.where(own == i, len_ref[i], own_len)
            at = mod(starts_of(own_ids) + slot, n) * ROWS + own * per + div(slot, n)
            place = jnp.where(slot < own_len, at, -1)
        half = (cut - done) // 2
        rows = lax.broadcasted_iota(jnp.int32, (LANES, rows_here), 0)
        for k in range(tiles):
            pick = jnp.where(rows + k * LANES == place, 1.0, 0.0).astype(jnp.bfloat16)
            moved = jnp.dot(pick, hid[:, done:cut], preferred_element_type=jnp.float32)
            moved = jnp.concatenate(
                [moved[:, :half].reshape(group, ROWS, half), moved[:, half:].reshape(group, ROWS, half)], axis=1
            )
            sends[c][k * group : (k + 1) * group] = moved.astype(jnp.bfloat16)

        @pl.loop(1, n)
        def _(k, c=c):
            block_copy(c, lax.rem(me + k, n), me).start()

        recvs[c][me] = sends[c][me]
        done = cut

    sub = lax.broadcasted_iota(jnp.int32, (ROWS, LANES), 0)
    lane8 = lax.broadcasted_iota(jnp.int32, (ROWS, LANES), 1)
    local = []
    for k in range(tiles):
        a_ids = jnp.zeros((ROWS, LANES), jnp.int32)
        a_len = jnp.zeros((ROWS, LANES), jnp.int32)
        for s in range(group):
            mine = (div(lane8, ROWS) == s) & (div(mod(lane8, ROWS), per) == sub)
            a_ids = jnp.where(mine, meta[k * group + s, ROWS:, :], a_ids)
            a_len = jnp.where(mine, meta[k * group + s, :ROWS, :], a_len)
        a_ids = jnp.sum(a_ids, axis=0, keepdims=True)
        a_len = jnp.sum(a_len, axis=0, keepdims=True)
        begin = starts_of(a_ids)
        t = mod(me - begin, n) + n * mod(lane1, per)
        local.append(jnp.where(t < a_len, div(begin + t, n), -1))

    out_rows = lax.broadcasted_iota(jnp.int32, (rows_here, LANES), 0)
    picks = [jnp.where(out_rows == spot, 1.0, 0.0).astype(jnp.bfloat16) for spot in local]
    wide = []
    for c in range(len(CUTS)):
        @pl.loop(1, n)
        def _(k, c=c):
            src = lax.rem(me + n - k, n)
            block_copy(c, src, src).wait_recv()

        total = None
        for k in range(tiles):
            got = recvs[c][k * group : (k + 1) * group].astype(jnp.float32)
            half = got.shape[2]
            got = jnp.concatenate(
                [got[:, :ROWS].reshape(LANES, half), got[:, ROWS:].reshape(LANES, half)], axis=1
            ).astype(jnp.bfloat16)
            more = jnp.dot(picks[k], got, preferred_element_type=jnp.float32)
            total = more if total is None else total + more
        wide.append(total)
    hidden = jnp.concatenate(wide, axis=1)
    loads[6].wait()
    normed = (
        hidden * lax.rsqrt(jnp.mean(hidden * hidden, axis=-1, keepdims=True) + 1e-06) * gain[...].reshape(1, width)
    ).astype(jnp.bfloat16)
    loads[7].wait()
    step = 256
    for at in range(0, w_up.shape[1], step):
        v = jnp.dot(normed, w_up[:, at : at + step], preferred_element_type=jnp.float32)
        act[:, at : at + step] = (v * (1.0 / (1.0 + jnp.exp(-v)))).astype(jnp.bfloat16)
    loads[8].wait()
    for at in range(0, width, step):
        v = jnp.dot(act[...], w_down[:, at : at + step], preferred_element_type=jnp.float32)
        out_ref[:, at : at + step] = (hidden[:, at : at + step] + v).astype(jnp.bfloat16)

    @pl.loop(1, n)
    def _(k):
        peer = lax.rem(me + k, n)
        meta_copy(peer, me).wait_send()
        for c in range(len(CUTS)):
            block_copy(c, peer, me).wait_send()


def local(new_qkv, cache_kv, resid, span_len, cache_len, series_perm, ff_gain, w_up, w_down):
    n = lax.axis_size("req")
    series, span, _ = new_qkv.shape
    cache, width, hidden = cache_kv.shape[1], resid.shape[2], w_up.shape[1]
    rows_here = series * span
    halves = [(b - a) // 2 for a, b in zip((0,) + CUTS, CUTS)]
    hbm, vmem = (pl.BlockSpec(memory_space=m) for m in (pltpu.HBM, pltpu.VMEM))
    return pl.pallas_call(
        functools.partial(kernel, n, series, span, cache, width),
        out_shape=jax.ShapeDtypeStruct((rows_here, width), jnp.bfloat16),
        in_specs=[hbm] * 9,
        out_specs=vmem,
        scratch_shapes=[
            pltpu.VMEM(new_qkv.shape, jnp.bfloat16),
            pltpu.VMEM(cache_kv.shape, jnp.bfloat16),
            pltpu.VMEM(resid.shape, jnp.bfloat16),
            pltpu.SMEM(span_len.shape, jnp.int32),
            pltpu.SMEM(cache_len.shape, jnp.int32),
            pltpu.SMEM(series_perm.shape, jnp.int32),
            pltpu.VMEM(ff_gain.shape, jnp.float32),
            pltpu.VMEM(w_up.shape, jnp.bfloat16),
            pltpu.VMEM(w_down.shape, jnp.bfloat16),
            pltpu.VMEM((rows_here, width), jnp.bfloat16),
            pltpu.VMEM((rows_here, hidden), jnp.bfloat16),
            pltpu.VMEM((2 * ROWS, LANES), jnp.int32),
            pltpu.VMEM((n, 2 * ROWS, LANES), jnp.int32),
            [pltpu.VMEM((n, 2 * ROWS, h), jnp.bfloat16) for h in halves],
            [pltpu.VMEM((n, 2 * ROWS, h), jnp.bfloat16) for h in halves],
            pltpu.SemaphoreType.DMA((9,)),
            pltpu.SemaphoreType.DMA((n,)),
            pltpu.SemaphoreType.DMA((n,)),
            pltpu.SemaphoreType.DMA((len(CUTS), n)),
            pltpu.SemaphoreType.DMA((len(CUTS), n)),
        ],
        compiler_params=pltpu.CompilerParams(
            collective_id=0, has_side_effects=True, vmem_limit_bytes=64 * 2**20
        ),
    )(new_qkv, cache_kv, resid, span_len, cache_len, series_perm, ff_gain, w_up, w_down)


def solution(mesh):
    rows3, rows1 = P(("grp", "req"), None, None), P(("grp", "req"))
    in_specs = (rows3, rows3, rows3, rows1, rows1, rows1, P(), P(), P())
    out_specs = P(("grp", "req"), None)
    return jax.shard_map(local, mesh=mesh, in_specs=in_specs, out_specs=out_specs, check_vma=False)
```

```python
import functools

import jax
import jax.numpy as jnp
from jax import lax
from jax.experimental import pallas as pl
from jax.experimental.pallas import tpu as pltpu
from jax.sharding import PartitionSpec as P

H = 16
LANES = 128
ROWS = 8
CUTS = (1280,)
HEAD_CUTS = (16,)


def div(x, k):
    return lax.shift_right_arithmetic(x, jnp.int32(k.bit_length() - 1)) if k & (k - 1) == 0 else x // k


def mod(x, k):
    return x & (k - 1) if k & (k - 1) == 0 else x % k


def windows(heads, head_size):
    found = []
    for h in heads:
        if found and (h + 1) * head_size <= found[-1][0] + 2 * LANES:
            found[-1][1].append(h)
        else:
            found.append((h * head_size // LANES * LANES, [h]))
    return found


def kernel(
    n, series, span, cache, width,
    qkv_hbm, cache_hbm, resid_hbm, len_hbm, clen_hbm, perm_hbm, gain_hbm, up_hbm, down_hbm,
    out_ref,
    qkv, ckv, resid, len_ref, clen_ref, perm_ref, gain, w_up, w_down, hid, act, meta_send, meta, sends, recvs,
    load_sem, meta_ssem, meta_rsem, ssems, rsems,
):
    me = lax.axis_index("req")
    head_size = width // H
    per = (span + n - 1) // n
    rows_here = series * span
    tiles = n * ROWS // LANES
    group = LANES // ROWS

    loads = [
        pltpu.make_async_copy(src, dst, load_sem.at[k])
        for k, (src, dst) in enumerate(
            (
                (len_hbm, len_ref), (perm_hbm, perm_ref), (clen_hbm, clen_ref), (qkv_hbm, qkv), (cache_hbm, ckv),
                (resid_hbm, resid), (gain_hbm, gain), (up_hbm, w_up), (down_hbm, w_down),
            )
        )
    ]
    barrier = pltpu.get_barrier_semaphore()

    @pl.loop(1, n, unroll=n <= 16)
    def _(k):
        pl.semaphore_signal(
            barrier, inc=1, device_id={"req": lax.rem(me + k, n)}, device_id_type=pl.DeviceIdType.MESH
        )

    for load in loads:
        load.start()
    for load in loads[:2]:
        load.wait()

    sub = lax.broadcasted_iota(jnp.int32, (ROWS, LANES), 0)
    lens = jnp.zeros((ROWS, LANES), jnp.int32)
    ids = jnp.zeros((ROWS, LANES), jnp.int32)
    for i in range(series):
        lens = jnp.where(sub == i, len_ref[i], lens)
        ids = jnp.where(sub == i, perm_ref[i], ids)
    meta_send[0:ROWS] = lens
    meta_send[ROWS:] = ids
    meta[me] = meta_send[...]
    pl.semaphore_wait(barrier, n - 1)

    def meta_copy(peer, slot):
        return pltpu.make_async_remote_copy(
            src_ref=meta_send, dst_ref=meta.at[slot], send_sem=meta_ssem.at[peer], recv_sem=meta_rsem.at[slot],
            device_id={"req": peer}, device_id_type=pl.DeviceIdType.MESH,
        )

    @pl.loop(1, n, unroll=n <= 16)
    def _(k):
        meta_copy(lax.rem(me + k, n), me).start()

    for load in loads[2:6]:
        load.wait()

    lane = lax.broadcasted_iota(jnp.int32, (1, 2 * LANES), 1)
    key_pos = lax.broadcasted_iota(jnp.int32, (span, cache + span), 1)
    row_pos = lax.broadcasted_iota(jnp.int32, (span, cache + span), 0)

    def attend(heads):
        wins = windows(heads, head_size)
        first, last = heads[0] * head_size, (heads[-1] + 1) * head_size

        @pl.loop(0, series)
        def _(i):
            limit = clen_ref[i]
            visible = (key_pos < limit) | ((key_pos >= cache) & (key_pos - cache <= row_pos))
            parts = {}
            for base, group_heads in wins:
                wide = min(2 * LANES, width - base)
                masks = [
                    jnp.where(
                        (lane[:, :wide] >= h * head_size - base) & (lane[:, :wide] < (h + 1) * head_size - base),
                        1.0, 0.0,
                    )
                    for h in group_heads
                ]
                q = qkv[i, :, base : base + wide]
                qs = jnp.concatenate([q * m.astype(jnp.bfloat16) for m in masks], axis=0)
                keys = jnp.concatenate(
                    [ckv[i, :, base : base + wide], qkv[i, :, width + base : width + base + wide]], axis=0
                )
                values = jnp.concatenate(
                    [ckv[i, :, width + base : width + base + wide],
                     qkv[i, :, 2 * width + base : 2 * width + base + wide]], axis=0
                )
                s = lax.dot_general(qs, keys, (((1,), (1,)), ((), ())), preferred_element_type=jnp.float32)
                s = s.reshape(len(masks), span, cache + span) * head_size ** (-0.5)
                s = jnp.where(visible[None], s, -1e30)
                e = jnp.exp(s - jnp.max(s, axis=-1, keepdims=True))
                w = (e * (1.0 / jnp.sum(e, axis=-1, keepdims=True))).astype(jnp.bfloat16)
                o = jnp.dot(
                    w.reshape(len(masks) * span, cache + span), values, preferred_element_type=jnp.float32
                )
                total = sum(o[k * span : (k + 1) * span] * m for k, m in enumerate(masks))
                for at in range(0, wide, LANES):
                    piece = total[:, at : at + LANES]
                    parts[base + at] = parts[base + at] + piece if base + at in parts else piece
            for at, piece in parts.items():
                if first <= at and at + LANES <= last:
                    hid[pl.ds(pl.multiple_of(i * span, span), span), at : at + LANES] = (
                        resid[i, :, at : at + LANES].astype(jnp.float32) + piece
                    ).astype(jnp.bfloat16)

    lane1 = lax.broadcasted_iota(jnp.int32, (1, LANES), 1)

    def starts_of(ids_of_lanes):
        earlier = jnp.where(meta[:, ROWS:, :] < ids_of_lanes[None], meta[:, :ROWS, :], 0)
        return jnp.sum(jnp.sum(earlier, axis=0), axis=0, keepdims=True)

    def block_copy(c, peer, slot):
        return pltpu.make_async_remote_copy(
            src_ref=sends[c].at[peer], dst_ref=recvs[c].at[slot], send_sem=ssems.at[c, peer],
            recv_sem=rsems.at[c, slot], device_id={"req": peer}, device_id_type=pl.DeviceIdType.MESH,
        )

    place = None
    done = 0
    for c, (head_end, cut) in enumerate(zip(HEAD_CUTS, CUTS)):
        attend(list(range(HEAD_CUTS[c - 1] if c else 0, head_end)))
        if c == 0:
            @pl.loop(1, n, unroll=n <= 16)
            def _(k):
                src = lax.rem(me + n - k, n)
                meta_copy(src, src).wait_recv()

            own_ids = jnp.zeros((1, rows_here), jnp.int32)
            own_len = jnp.zeros((1, rows_here), jnp.int32)
            token = lax.broadcasted_iota(jnp.int32, (1, rows_here), 1)
            own = div(token, span)
            slot = mod(token, span)
            for i in range(series):
                own_ids = jnp.where(own == i, perm_ref[i], own_ids)
                own_len = jnp.where(own == i, len_ref[i], own_len)
            at = mod(starts_of(own_ids) + slot, n) * ROWS + own * per + div(slot, n)
            place = jnp.where(slot < own_len, at, -1)
        half = (cut - done) // 2
        rows = lax.broadcasted_iota(jnp.int32, (LANES, rows_here), 0)
        for k in range(tiles):
            pick = jnp.where(rows + k * LANES == place, 1.0, 0.0).astype(jnp.bfloat16)
            moved = jnp.dot(pick, hid[:, done:cut], preferred_element_type=jnp.float32)
            moved = jnp.concatenate(
                [moved[:, :half].reshape(group, ROWS, half), moved[:, half:].reshape(group, ROWS, half)], axis=1
            )
            sends[c][k * group : (k + 1) * group] = moved.astype(jnp.bfloat16)

        @pl.loop(1, n, unroll=n <= 16)
        def _(k, c=c):
            block_copy(c, lax.rem(me + k, n), me).start()

        recvs[c][me] = sends[c][me]
        done = cut

    sub = lax.broadcasted_iota(jnp.int32, (ROWS, LANES), 0)
    lane8 = lax.broadcasted_iota(jnp.int32, (ROWS, LANES), 1)
    local = []
    for k in range(tiles):
        a_ids = jnp.zeros((ROWS, LANES), jnp.int32)
        a_len = jnp.zeros((ROWS, LANES), jnp.int32)
        for s in range(group):
            mine = (div(lane8, ROWS) == s) & (div(mod(lane8, ROWS), per) == sub)
            a_ids = jnp.where(mine, meta[k * group + s, ROWS:, :], a_ids)
            a_len = jnp.where(mine, meta[k * group + s, :ROWS, :], a_len)
        a_ids = jnp.sum(a_ids, axis=0, keepdims=True)
        a_len = jnp.sum(a_len, axis=0, keepdims=True)
        begin = starts_of(a_ids)
        t = mod(me - begin, n) + n * mod(lane1, per)
        local.append(jnp.where(t < a_len, div(begin + t, n), -1))

    out_rows = lax.broadcasted_iota(jnp.int32, (rows_here, LANES), 0)
    picks = [jnp.where(out_rows == spot, 1.0, 0.0).astype(jnp.bfloat16) for spot in local]
    wide = []
    for c in range(len(CUTS)):
        @pl.loop(1, n, unroll=n <= 16)
        def _(k, c=c):
            src = lax.rem(me + n - k, n)
            block_copy(c, src, src).wait_recv()

        total = None
        for k in range(tiles):
            got = recvs[c][k * group : (k + 1) * group].astype(jnp.float32)
            half = got.shape[2]
            got = jnp.concatenate(
                [got[:, :ROWS].reshape(LANES, half), got[:, ROWS:].reshape(LANES, half)], axis=1
            ).astype(jnp.bfloat16)
            more = jnp.dot(picks[k], got, preferred_element_type=jnp.float32)
            total = more if total is None else total + more
        wide.append(total)
    hidden = jnp.concatenate(wide, axis=1)
    loads[6].wait()
    normed = (
        hidden * lax.rsqrt(jnp.mean(hidden * hidden, axis=-1, keepdims=True) + 1e-06) * gain[...].reshape(1, width)
    ).astype(jnp.bfloat16)
    loads[7].wait()
    step = 256
    for at in range(0, w_up.shape[1], step):
        v = jnp.dot(normed, w_up[:, at : at + step], preferred_element_type=jnp.float32)
        act[:, at : at + step] = (v * (1.0 / (1.0 + jnp.exp(-v)))).astype(jnp.bfloat16)
    loads[8].wait()
    for at in range(0, width, step):
        v = jnp.dot(act[...], w_down[:, at : at + step], preferred_element_type=jnp.float32)
        out_ref[:, at : at + step] = (hidden[:, at : at + step] + v).astype(jnp.bfloat16)

    @pl.loop(1, n, unroll=n <= 16)
    def _(k):
        peer = lax.rem(me + k, n)
        meta_copy(peer, me).wait_send()
        for c in range(len(CUTS)):
            block_copy(c, peer, me).wait_send()


def local(new_qkv, cache_kv, resid, span_len, cache_len, series_perm, ff_gain, w_up, w_down):
    n = lax.axis_size("req")
    series, span, _ = new_qkv.shape
    cache, width, hidden = cache_kv.shape[1], resid.shape[2], w_up.shape[1]
    rows_here = series * span
    halves = [(b - a) // 2 for a, b in zip((0,) + CUTS, CUTS)]
    hbm, vmem = (pl.BlockSpec(memory_space=m) for m in (pltpu.HBM, pltpu.VMEM))
    return pl.pallas_call(
        functools.partial(kernel, n, series, span, cache, width),
        out_shape=jax.ShapeDtypeStruct((rows_here, width), jnp.bfloat16),
        in_specs=[hbm] * 9,
        out_specs=vmem,
        scratch_shapes=[
            pltpu.VMEM(new_qkv.shape, jnp.bfloat16),
            pltpu.VMEM(cache_kv.shape, jnp.bfloat16),
            pltpu.VMEM(resid.shape, jnp.bfloat16),
            pltpu.SMEM(span_len.shape, jnp.int32),
            pltpu.SMEM(cache_len.shape, jnp.int32),
            pltpu.SMEM(series_perm.shape, jnp.int32),
            pltpu.VMEM(ff_gain.shape, jnp.float32),
            pltpu.VMEM(w_up.shape, jnp.bfloat16),
            pltpu.VMEM(w_down.shape, jnp.bfloat16),
            pltpu.VMEM((rows_here, width), jnp.bfloat16),
            pltpu.VMEM((rows_here, hidden), jnp.bfloat16),
            pltpu.VMEM((2 * ROWS, LANES), jnp.int32),
            pltpu.VMEM((n, 2 * ROWS, LANES), jnp.int32),
            [pltpu.VMEM((n, 2 * ROWS, h), jnp.bfloat16) for h in halves],
            [pltpu.VMEM((n, 2 * ROWS, h), jnp.bfloat16) for h in halves],
            pltpu.SemaphoreType.DMA((9,)),
            pltpu.SemaphoreType.DMA((n,)),
            pltpu.SemaphoreType.DMA((n,)),
            pltpu.SemaphoreType.DMA((len(CUTS), n)),
            pltpu.SemaphoreType.DMA((len(CUTS), n)),
        ],
        compiler_params=pltpu.CompilerParams(
            collective_id=0, has_side_effects=True, vmem_limit_bytes=64 * 2**20
        ),
    )(new_qkv, cache_kv, resid, span_len, cache_len, series_perm, ff_gain, w_up, w_down)


def solution(mesh):
    rows3, rows1 = P(("grp", "req"), None, None), P(("grp", "req"))
    in_specs = (rows3, rows3, rows3, rows1, rows1, rows1, P(), P(), P())
    out_specs = P(("grp", "req"), None)
    return jax.shard_map(local, mesh=mesh, in_specs=in_specs, out_specs=out_specs, check_vma=False)
```

```python
import functools

import jax
import jax.numpy as jnp
from jax import lax
from jax.experimental import pallas as pl
from jax.experimental.pallas import tpu as pltpu
from jax.sharding import PartitionSpec as P

H = 16
LANES = 128
ROWS = 8
CUTS = (1280,)


def div(x, k):
    return lax.shift_right_arithmetic(x, jnp.int32(k.bit_length() - 1)) if k & (k - 1) == 0 else x // k


def mod(x, k):
    return x & (k - 1) if k & (k - 1) == 0 else x % k


def windows(heads, head_size):
    found = []
    for h in heads:
        if found and (h + 1) * head_size <= found[-1][0] + 2 * LANES:
            found[-1][1].append(h)
        else:
            found.append((h * head_size // LANES * LANES, [h]))
    return found


def kernel(
    n, series, span, cache, width,
    qkv_hbm, cache_hbm, resid_hbm, len_hbm, clen_hbm, perm_hbm, gain_hbm, up_hbm, down_hbm,
    out_ref,
    qkv, ckv, resid, len_ref, clen_ref, perm_ref, gain, w_up, w_down, hid, act, meta_send, meta, sends, recvs,
    load_sem, meta_ssem, meta_rsem, ssems, rsems,
):
    me = lax.axis_index("req")
    head_size = width // H
    per = (span + n - 1) // n
    rows_here = series * span
    tiles = n * ROWS // LANES
    group = LANES // ROWS

    loads = [
        pltpu.make_async_copy(src, dst, load_sem.at[k])
        for k, (src, dst) in enumerate(
            (
                (len_hbm, len_ref), (perm_hbm, perm_ref), (clen_hbm, clen_ref), (qkv_hbm, qkv), (cache_hbm, ckv),
                (resid_hbm, resid), (gain_hbm, gain), (up_hbm, w_up), (down_hbm, w_down),
            )
        )
    ]
    barrier = pltpu.get_barrier_semaphore()

    @pl.loop(1, n, unroll=n <= 16)
    def _(k):
        pl.semaphore_signal(
            barrier, inc=1, device_id={"req": lax.rem(me + k, n)}, device_id_type=pl.DeviceIdType.MESH
        )

    for load in loads:
        load.start()
    for load in loads[:2]:
        load.wait()

    sub = lax.broadcasted_iota(jnp.int32, (ROWS, LANES), 0)
    lens = jnp.zeros((ROWS, LANES), jnp.int32)
    ids = jnp.zeros((ROWS, LANES), jnp.int32)
    for i in range(series):
        lens = jnp.where(sub == i, len_ref[i], lens)
        ids = jnp.where(sub == i, perm_ref[i], ids)
    meta_send[0:ROWS] = lens
    meta_send[ROWS:] = ids
    meta[me] = meta_send[...]

    def meta_copy(peer, slot):
        return pltpu.make_async_remote_copy(
            src_ref=meta_send, dst_ref=meta.at[slot], send_sem=meta_ssem.at[peer], recv_sem=meta_rsem.at[slot],
            device_id={"req": peer}, device_id_type=pl.DeviceIdType.MESH,
        )

    for load in loads[2:6]:
        load.wait()

    lane = lax.broadcasted_iota(jnp.int32, (1, 2 * LANES), 1)
    key_pos = lax.broadcasted_iota(jnp.int32, (span, cache + span), 1)
    row_pos = lax.broadcasted_iota(jnp.int32, (span, cache + span), 0)

    def attend(heads):
        wins = windows(heads, head_size)
        first, last = heads[0] * head_size, (heads[-1] + 1) * head_size

        @pl.loop(0, series, unroll=2)
        def _(i):
            limit = clen_ref[i]
            visible = (key_pos < limit) | ((key_pos >= cache) & (key_pos - cache <= row_pos))
            parts = {}
            for base, group_heads in wins:
                wide = min(2 * LANES, width - base)
                masks = [
                    jnp.where(
                        (lane[:, :wide] >= h * head_size - base) & (lane[:, :wide] < (h + 1) * head_size - base),
                        1.0, 0.0,
                    )
                    for h in group_heads
                ]
                q = qkv[i, :, base : base + wide]
                qs = jnp.concatenate([q * m.astype(jnp.bfloat16) for m in masks], axis=0)
                keys = jnp.concatenate(
                    [ckv[i, :, base : base + wide], qkv[i, :, width + base : width + base + wide]], axis=0
                )
                values = jnp.concatenate(
                    [ckv[i, :, width + base : width + base + wide],
                     qkv[i, :, 2 * width + base : 2 * width + base + wide]], axis=0
                )
                s = lax.dot_general(qs, keys, (((1,), (1,)), ((), ())), preferred_element_type=jnp.float32)
                s = s.reshape(len(masks), span, cache + span) * head_size ** (-0.5)
                s = jnp.where(visible[None], s, -1e30)
                e = jnp.exp(s - jnp.max(s, axis=-1, keepdims=True))
                w = (e * (1.0 / jnp.sum(e, axis=-1, keepdims=True))).astype(jnp.bfloat16)
                o = jnp.dot(
                    w.reshape(len(masks) * span, cache + span), values, preferred_element_type=jnp.float32
                )
                total = sum(o[k * span : (k + 1) * span] * m for k, m in enumerate(masks))
                for at in range(0, wide, LANES):
                    piece = total[:, at : at + LANES]
                    parts[base + at] = parts[base + at] + piece if base + at in parts else piece
            for at, piece in parts.items():
                if first <= at and at + LANES <= last:
                    hid[pl.ds(pl.multiple_of(i * span, span), span), at : at + LANES] = (
                        resid[i, :, at : at + LANES].astype(jnp.float32) + piece
                    ).astype(jnp.bfloat16)

    lane1 = lax.broadcasted_iota(jnp.int32, (1, LANES), 1)

    def starts_of(ids_of_lanes):
        earlier = jnp.where(meta[:, ROWS:, :] < ids_of_lanes[None], meta[:, :ROWS, :], 0)
        return jnp.sum(jnp.sum(earlier, axis=0), axis=0, keepdims=True)

    def block_copy(c, peer, slot):
        return pltpu.make_async_remote_copy(
            src_ref=sends[c].at[peer], dst_ref=recvs[c].at[slot], send_sem=ssems.at[c, peer],
            recv_sem=rsems.at[c, slot], device_id={"req": peer}, device_id_type=pl.DeviceIdType.MESH,
        )

    pl.semaphore_wait(barrier, n - 1)

    @pl.loop(1, n, unroll=n <= 16)
    def _(k):
        meta_copy(lax.rem(me + k, n), me).start()

    attend(list(range(H)))
    loads[6].wait()
    hidden = hid[...].astype(jnp.float32)
    normed = (
        hidden * lax.rsqrt(jnp.mean(hidden * hidden, axis=-1, keepdims=True) + 1e-06) * gain[...].reshape(1, width)
    ).astype(jnp.bfloat16)
    loads[7].wait()
    step = 256
    for at in range(0, w_up.shape[1], step):
        v = jnp.dot(normed, w_up[:, at : at + step], preferred_element_type=jnp.float32)
        act[:, at : at + step] = (v * (1.0 / (1.0 + jnp.exp(-v)))).astype(jnp.bfloat16)
    loads[8].wait()
    for at in range(0, width, step):
        v = jnp.dot(act[...], w_down[:, at : at + step], preferred_element_type=jnp.float32)
        hid[:, at : at + step] = (hid[:, at : at + step].astype(jnp.float32) + v).astype(jnp.bfloat16)

    place = None
    done = 0
    for c, cut in enumerate(CUTS):
        if c == 0:
            @pl.loop(1, n, unroll=n <= 16)
            def _(k):
                src = lax.rem(me + n - k, n)
                meta_copy(src, src).wait_recv()

            own_ids = jnp.zeros((1, rows_here), jnp.int32)
            own_len = jnp.zeros((1, rows_here), jnp.int32)
            token = lax.broadcasted_iota(jnp.int32, (1, rows_here), 1)
            own = div(token, span)
            slot = mod(token, span)
            for i in range(series):
                own_ids = jnp.where(own == i, perm_ref[i], own_ids)
                own_len = jnp.where(own == i, len_ref[i], own_len)
            at = mod(starts_of(own_ids) + slot, n) * ROWS + own * per + div(slot, n)
            place = jnp.where(slot < own_len, at, -1)
        half = (cut - done) // 2
        rows = lax.broadcasted_iota(jnp.int32, (LANES, rows_here), 0)
        for k in range(tiles):
            pick = jnp.where(rows + k * LANES == place, 1.0, 0.0).astype(jnp.bfloat16)
            moved = jnp.dot(pick, hid[:, done:cut], preferred_element_type=jnp.float32)
            moved = jnp.concatenate(
                [moved[:, :half].reshape(group, ROWS, half), moved[:, half:].reshape(group, ROWS, half)], axis=1
            )
            sends[c][k * group : (k + 1) * group] = moved.astype(jnp.bfloat16)

        @pl.loop(1, n, unroll=n <= 16)
        def _(k, c=c):
            block_copy(c, lax.rem(me + k, n), me).start()

        recvs[c][me] = sends[c][me]
        done = cut

    sub = lax.broadcasted_iota(jnp.int32, (ROWS, LANES), 0)
    lane8 = lax.broadcasted_iota(jnp.int32, (ROWS, LANES), 1)
    local = []
    for k in range(tiles):
        a_ids = jnp.zeros((ROWS, LANES), jnp.int32)
        a_len = jnp.zeros((ROWS, LANES), jnp.int32)
        for s in range(group):
            mine = (div(lane8, ROWS) == s) & (div(mod(lane8, ROWS), per) == sub)
            a_ids = jnp.where(mine, meta[k * group + s, ROWS:, :], a_ids)
            a_len = jnp.where(mine, meta[k * group + s, :ROWS, :], a_len)
        a_ids = jnp.sum(a_ids, axis=0, keepdims=True)
        a_len = jnp.sum(a_len, axis=0, keepdims=True)
        begin = starts_of(a_ids)
        t = mod(me - begin, n) + n * mod(lane1, per)
        local.append(jnp.where(t < a_len, div(begin + t, n), -1))

    out_rows = lax.broadcasted_iota(jnp.int32, (rows_here, LANES), 0)
    picks = [jnp.where(out_rows == spot, 1.0, 0.0).astype(jnp.bfloat16) for spot in local]
    for c in range(len(CUTS)):
        @pl.loop(1, n, unroll=n <= 16)
        def _(k, c=c):
            src = lax.rem(me + n - k, n)
            block_copy(c, src, src).wait_recv()

        total = None
        for k in range(tiles):
            got = recvs[c][k * group : (k + 1) * group].astype(jnp.float32)
            half = got.shape[2]
            got = jnp.concatenate(
                [got[:, :ROWS].reshape(LANES, half), got[:, ROWS:].reshape(LANES, half)], axis=1
            ).astype(jnp.bfloat16)
            more = jnp.dot(picks[k], got, preferred_element_type=jnp.float32)
            total = more if total is None else total + more
        out_ref[:, (CUTS[c - 1] if c else 0) : CUTS[c]] = total.astype(jnp.bfloat16)

    @pl.loop(1, n, unroll=n <= 16)
    def _(k):
        peer = lax.rem(me + k, n)
        meta_copy(peer, me).wait_send()
        for c in range(len(CUTS)):
            block_copy(c, peer, me).wait_send()


def local(new_qkv, cache_kv, resid, span_len, cache_len, series_perm, ff_gain, w_up, w_down):
    n = lax.axis_size("req")
    series, span, _ = new_qkv.shape
    cache, width, hidden = cache_kv.shape[1], resid.shape[2], w_up.shape[1]
    rows_here = series * span
    halves = [(b - a) // 2 for a, b in zip((0,) + CUTS, CUTS)]
    hbm, vmem = (pl.BlockSpec(memory_space=m) for m in (pltpu.HBM, pltpu.VMEM))
    return pl.pallas_call(
        functools.partial(kernel, n, series, span, cache, width),
        out_shape=jax.ShapeDtypeStruct((rows_here, width), jnp.bfloat16),
        in_specs=[hbm] * 9,
        out_specs=vmem,
        scratch_shapes=[
            pltpu.VMEM(new_qkv.shape, jnp.bfloat16),
            pltpu.VMEM(cache_kv.shape, jnp.bfloat16),
            pltpu.VMEM(resid.shape, jnp.bfloat16),
            pltpu.SMEM(span_len.shape, jnp.int32),
            pltpu.SMEM(cache_len.shape, jnp.int32),
            pltpu.SMEM(series_perm.shape, jnp.int32),
            pltpu.VMEM(ff_gain.shape, jnp.float32),
            pltpu.VMEM(w_up.shape, jnp.bfloat16),
            pltpu.VMEM(w_down.shape, jnp.bfloat16),
            pltpu.VMEM((rows_here, width), jnp.bfloat16),
            pltpu.VMEM((rows_here, hidden), jnp.bfloat16),
            pltpu.VMEM((2 * ROWS, LANES), jnp.int32),
            pltpu.VMEM((n, 2 * ROWS, LANES), jnp.int32),
            [pltpu.VMEM((n, 2 * ROWS, h), jnp.bfloat16) for h in halves],
            [pltpu.VMEM((n, 2 * ROWS, h), jnp.bfloat16) for h in halves],
            pltpu.SemaphoreType.DMA((9,)),
            pltpu.SemaphoreType.DMA((n,)),
            pltpu.SemaphoreType.DMA((n,)),
            pltpu.SemaphoreType.DMA((len(CUTS), n)),
            pltpu.SemaphoreType.DMA((len(CUTS), n)),
        ],
        compiler_params=pltpu.CompilerParams(
            collective_id=0, has_side_effects=True, vmem_limit_bytes=64 * 2**20
        ),
    )(new_qkv, cache_kv, resid, span_len, cache_len, series_perm, ff_gain, w_up, w_down)


def solution(mesh):
    rows3, rows1 = P(("grp", "req"), None, None), P(("grp", "req"))
    in_specs = (rows3, rows3, rows3, rows1, rows1, rows1, P(), P(), P())
    out_specs = P(("grp", "req"), None)
    return jax.shard_map(local, mesh=mesh, in_specs=in_specs, out_specs=out_specs, check_vma=False)
```

```python
import functools

import jax
import jax.numpy as jnp
from jax import lax
from jax.experimental import pallas as pl
from jax.experimental.pallas import tpu as pltpu
from jax.sharding import PartitionSpec as P

H = 16
LANES = 128
ROWS = 8
CUTS = (1280,)


def div(x, k):
    return lax.shift_right_arithmetic(x, jnp.int32(k.bit_length() - 1)) if k & (k - 1) == 0 else x // k


def mod(x, k):
    return x & (k - 1) if k & (k - 1) == 0 else x % k


def windows(heads, head_size):
    found = []
    for h in heads:
        if found and (h + 1) * head_size <= found[-1][0] + 2 * LANES:
            found[-1][1].append(h)
        else:
            found.append((h * head_size // LANES * LANES, [h]))
    return found


def kernel(
    n, series, span, cache, width,
    qkv_hbm, cache_hbm, resid_hbm, len_hbm, clen_hbm, perm_hbm, gain_hbm, up_hbm, down_hbm,
    out_ref,
    qkv, ckv, resid, len_ref, clen_ref, perm_ref, gain, w_up, w_down, hid, act, meta_send, meta, sends, recvs,
    load_sem, meta_ssem, meta_rsem, ssems, rsems,
):
    me = lax.axis_index("req")
    head_size = width // H
    per = (span + n - 1) // n
    rows_here = series * span
    tiles = n * ROWS // LANES
    group = LANES // ROWS

    loads = [
        pltpu.make_async_copy(src, dst, load_sem.at[k])
        for k, (src, dst) in enumerate(
            (
                (len_hbm, len_ref), (perm_hbm, perm_ref), (clen_hbm, clen_ref), (qkv_hbm, qkv), (cache_hbm, ckv),
                (resid_hbm, resid), (gain_hbm, gain), (up_hbm, w_up), (down_hbm, w_down),
            )
        )
    ]
    barrier = pltpu.get_barrier_semaphore()

    @pl.loop(1, n, unroll=n <= 16)
    def _(k):
        pl.semaphore_signal(
            barrier, inc=1, device_id={"req": lax.rem(me + k, n)}, device_id_type=pl.DeviceIdType.MESH
        )

    for load in loads:
        load.start()
    for load in loads[:2]:
        load.wait()

    sub = lax.broadcasted_iota(jnp.int32, (ROWS, LANES), 0)
    lens = jnp.zeros((ROWS, LANES), jnp.int32)
    ids = jnp.zeros((ROWS, LANES), jnp.int32)
    for i in range(series):
        lens = jnp.where(sub == i, len_ref[i], lens)
        ids = jnp.where(sub == i, perm_ref[i], ids)
    meta_send[0:ROWS] = lens
    meta_send[ROWS:] = ids
    meta[me] = meta_send[...]

    def meta_copy(peer, slot):
        return pltpu.make_async_remote_copy(
            src_ref=meta_send, dst_ref=meta.at[slot], send_sem=meta_ssem.at[peer], recv_sem=meta_rsem.at[slot],
            device_id={"req": peer}, device_id_type=pl.DeviceIdType.MESH,
        )

    for load in loads[2:6]:
        load.wait()

    lane = lax.broadcasted_iota(jnp.int32, (1, 2 * LANES), 1)
    key_pos = lax.broadcasted_iota(jnp.int32, (span, cache + span), 1)
    row_pos = lax.broadcasted_iota(jnp.int32, (span, cache + span), 0)

    def attend(heads):
        wins = windows(heads, head_size)
        first, last = heads[0] * head_size, (heads[-1] + 1) * head_size

        @pl.loop(0, series, unroll=True)
        def _(i):
            limit = clen_ref[i]
            visible = (key_pos < limit) | ((key_pos >= cache) & (key_pos - cache <= row_pos))
            parts = {}
            for base, group_heads in wins:
                wide = min(2 * LANES, width - base)
                masks = [
                    jnp.where(
                        (lane[:, :wide] >= h * head_size - base) & (lane[:, :wide] < (h + 1) * head_size - base),
                        1.0, 0.0,
                    )
                    for h in group_heads
                ]
                q = qkv[i, :, base : base + wide]
                qs = jnp.concatenate([q * m.astype(jnp.bfloat16) for m in masks], axis=0)
                keys = jnp.concatenate(
                    [ckv[i, :, base : base + wide], qkv[i, :, width + base : width + base + wide]], axis=0
                )
                values = jnp.concatenate(
                    [ckv[i, :, width + base : width + base + wide],
                     qkv[i, :, 2 * width + base : 2 * width + base + wide]], axis=0
                )
                s = lax.dot_general(qs, keys, (((1,), (1,)), ((), ())), preferred_element_type=jnp.float32)
                s = s.reshape(len(masks), span, cache + span) * head_size ** (-0.5)
                s = jnp.where(visible[None], s, -1e30)
                e = jnp.exp(s - jnp.max(s, axis=-1, keepdims=True))
                w = (e * (1.0 / jnp.sum(e, axis=-1, keepdims=True))).astype(jnp.bfloat16)
                o = jnp.dot(
                    w.reshape(len(masks) * span, cache + span), values, preferred_element_type=jnp.float32
                )
                total = sum(o[k * span : (k + 1) * span] * m for k, m in enumerate(masks))
                for at in range(0, wide, LANES):
                    piece = total[:, at : at + LANES]
                    parts[base + at] = parts[base + at] + piece if base + at in parts else piece
            for at, piece in parts.items():
                if first <= at and at + LANES <= last:
                    hid[pl.ds(pl.multiple_of(i * span, span), span), at : at + LANES] = (
                        resid[i, :, at : at + LANES].astype(jnp.float32) + piece
                    ).astype(jnp.bfloat16)

    lane1 = lax.broadcasted_iota(jnp.int32, (1, LANES), 1)

    def starts_of(ids_of_lanes):
        earlier = jnp.where(meta[:, ROWS:, :] < ids_of_lanes[None], meta[:, :ROWS, :], 0)
        return jnp.sum(jnp.sum(earlier, axis=0), axis=0, keepdims=True)

    def block_copy(c, peer, slot):
        return pltpu.make_async_remote_copy(
            src_ref=sends[c].at[peer], dst_ref=recvs[c].at[slot], send_sem=ssems.at[c, peer],
            recv_sem=rsems.at[c, slot], device_id={"req": peer}, device_id_type=pl.DeviceIdType.MESH,
        )

    pl.semaphore_wait(barrier, n - 1)

    @pl.loop(1, n, unroll=n <= 16)
    def _(k):
        meta_copy(lax.rem(me + k, n), me).start()

    attend(list(range(H)))
    loads[6].wait()
    hidden = hid[...].astype(jnp.float32)
    normed = (
        hidden * lax.rsqrt(jnp.mean(hidden * hidden, axis=-1, keepdims=True) + 1e-06) * gain[...].reshape(1, width)
    ).astype(jnp.bfloat16)
    loads[7].wait()
    step = 256
    for at in range(0, w_up.shape[1], step):
        v = jnp.dot(normed, w_up[:, at : at + step], preferred_element_type=jnp.float32)
        act[:, at : at + step] = (v * (1.0 / (1.0 + jnp.exp(-v)))).astype(jnp.bfloat16)
    loads[8].wait()
    for at in range(0, width, step):
        v = jnp.dot(act[...], w_down[:, at : at + step], preferred_element_type=jnp.float32)
        hid[:, at : at + step] = (hid[:, at : at + step].astype(jnp.float32) + v).astype(jnp.bfloat16)

    place = None
    done = 0
    for c, cut in enumerate(CUTS):
        if c == 0:
            @pl.loop(1, n, unroll=n <= 16)
            def _(k):
                src = lax.rem(me + n - k, n)
                meta_copy(src, src).wait_recv()

            own_ids = jnp.zeros((1, rows_here), jnp.int32)
            own_len = jnp.zeros((1, rows_here), jnp.int32)
            token = lax.broadcasted_iota(jnp.int32, (1, rows_here), 1)
            own = div(token, span)
            slot = mod(token, span)
            for i in range(series):
                own_ids = jnp.where(own == i, perm_ref[i], own_ids)
                own_len = jnp.where(own == i, len_ref[i], own_len)
            at = mod(starts_of(own_ids) + slot, n) * ROWS + own * per + div(slot, n)
            place = jnp.where(slot < own_len, at, -1)
        half = (cut - done) // 2
        rows = lax.broadcasted_iota(jnp.int32, (LANES, rows_here), 0)
        for k in range(tiles):
            pick = jnp.where(rows + k * LANES == place, 1.0, 0.0).astype(jnp.bfloat16)
            moved = jnp.dot(pick, hid[:, done:cut], preferred_element_type=jnp.float32)
            moved = jnp.concatenate(
                [moved[:, :half].reshape(group, ROWS, half), moved[:, half:].reshape(group, ROWS, half)], axis=1
            )
            sends[c][k * group : (k + 1) * group] = moved.astype(jnp.bfloat16)

        @pl.loop(1, n, unroll=n <= 16)
        def _(k, c=c):
            block_copy(c, lax.rem(me + k, n), me).start()

        recvs[c][me] = sends[c][me]
        done = cut

    sub = lax.broadcasted_iota(jnp.int32, (ROWS, LANES), 0)
    lane8 = lax.broadcasted_iota(jnp.int32, (ROWS, LANES), 1)
    local = []
    for k in range(tiles):
        a_ids = jnp.zeros((ROWS, LANES), jnp.int32)
        a_len = jnp.zeros((ROWS, LANES), jnp.int32)
        for s in range(group):
            mine = (div(lane8, ROWS) == s) & (div(mod(lane8, ROWS), per) == sub)
            a_ids = jnp.where(mine, meta[k * group + s, ROWS:, :], a_ids)
            a_len = jnp.where(mine, meta[k * group + s, :ROWS, :], a_len)
        a_ids = jnp.sum(a_ids, axis=0, keepdims=True)
        a_len = jnp.sum(a_len, axis=0, keepdims=True)
        begin = starts_of(a_ids)
        t = mod(me - begin, n) + n * mod(lane1, per)
        local.append(jnp.where(t < a_len, div(begin + t, n), -1))

    out_rows = lax.broadcasted_iota(jnp.int32, (rows_here, LANES), 0)
    picks = [jnp.where(out_rows == spot, 1.0, 0.0).astype(jnp.bfloat16) for spot in local]
    for c in range(len(CUTS)):
        @pl.loop(1, n, unroll=n <= 16)
        def _(k, c=c):
            src = lax.rem(me + n - k, n)
            block_copy(c, src, src).wait_recv()

        total = None
        for k in range(tiles):
            got = recvs[c][k * group : (k + 1) * group].astype(jnp.float32)
            half = got.shape[2]
            got = jnp.concatenate(
                [got[:, :ROWS].reshape(LANES, half), got[:, ROWS:].reshape(LANES, half)], axis=1
            ).astype(jnp.bfloat16)
            more = jnp.dot(picks[k], got, preferred_element_type=jnp.float32)
            total = more if total is None else total + more
        out_ref[:, (CUTS[c - 1] if c else 0) : CUTS[c]] = total.astype(jnp.bfloat16)

    @pl.loop(1, n, unroll=n <= 16)
    def _(k):
        peer = lax.rem(me + k, n)
        meta_copy(peer, me).wait_send()
        for c in range(len(CUTS)):
            block_copy(c, peer, me).wait_send()


def local(new_qkv, cache_kv, resid, span_len, cache_len, series_perm, ff_gain, w_up, w_down):
    n = lax.axis_size("req")
    series, span, _ = new_qkv.shape
    cache, width, hidden = cache_kv.shape[1], resid.shape[2], w_up.shape[1]
    rows_here = series * span
    halves = [(b - a) // 2 for a, b in zip((0,) + CUTS, CUTS)]
    hbm, vmem = (pl.BlockSpec(memory_space=m) for m in (pltpu.HBM, pltpu.VMEM))
    return pl.pallas_call(
        functools.partial(kernel, n, series, span, cache, width),
        out_shape=jax.ShapeDtypeStruct((rows_here, width), jnp.bfloat16),
        in_specs=[hbm] * 9,
        out_specs=vmem,
        scratch_shapes=[
            pltpu.VMEM(new_qkv.shape, jnp.bfloat16),
            pltpu.VMEM(cache_kv.shape, jnp.bfloat16),
            pltpu.VMEM(resid.shape, jnp.bfloat16),
            pltpu.SMEM(span_len.shape, jnp.int32),
            pltpu.SMEM(cache_len.shape, jnp.int32),
            pltpu.SMEM(series_perm.shape, jnp.int32),
            pltpu.VMEM(ff_gain.shape, jnp.float32),
            pltpu.VMEM(w_up.shape, jnp.bfloat16),
            pltpu.VMEM(w_down.shape, jnp.bfloat16),
            pltpu.VMEM((rows_here, width), jnp.bfloat16),
            pltpu.VMEM((rows_here, hidden), jnp.bfloat16),
            pltpu.VMEM((2 * ROWS, LANES), jnp.int32),
            pltpu.VMEM((n, 2 * ROWS, LANES), jnp.int32),
            [pltpu.VMEM((n, 2 * ROWS, h), jnp.bfloat16) for h in halves],
            [pltpu.VMEM((n, 2 * ROWS, h), jnp.bfloat16) for h in halves],
            pltpu.SemaphoreType.DMA((9,)),
            pltpu.SemaphoreType.DMA((n,)),
            pltpu.SemaphoreType.DMA((n,)),
            pltpu.SemaphoreType.DMA((len(CUTS), n)),
            pltpu.SemaphoreType.DMA((len(CUTS), n)),
        ],
        compiler_params=pltpu.CompilerParams(
            collective_id=0, has_side_effects=True, vmem_limit_bytes=64 * 2**20
        ),
    )(new_qkv, cache_kv, resid, span_len, cache_len, series_perm, ff_gain, w_up, w_down)


def solution(mesh):
    rows3, rows1 = P(("grp", "req"), None, None), P(("grp", "req"))
    in_specs = (rows3, rows3, rows3, rows1, rows1, rows1, P(), P(), P())
    out_specs = P(("grp", "req"), None)
    return jax.shard_map(local, mesh=mesh, in_specs=in_specs, out_specs=out_specs, check_vma=False)
```
